32 devices in a mesh: grp: 2 (over y), seq: 8 (over z, x), head: 2 (over core).
Axes of the slice: x: 2, y: 2, z: 4, core: 2. Of those that a mesh axis runs over, the one named last changes fastest.
Arguments:
- queries: bfloat16 [8192, 1024], P(('grp', 'seq'), 'head'), parts along dimension 0, may hold values from -7 to 7
- keys: bfloat16 [8192, 1024], P(('grp', 'seq'), 'head'), parts along dimension 0, may hold values from -4 to 4
- values: bfloat16 [8192, 1024], P(('grp', 'seq'), 'head'), parts along dimension 0, may hold values from -6 to 6
- grad_out: bfloat16 [8192, 1024], P(('grp', 'seq'), 'head'), parts along dimension 0, may hold values from -6 to 6
- table_lengths: int32 [32], P('grp'), parts along dimension 0, may hold values from 1 to 32, 64 in all
- table_cols: int32 [32], P('grp'), parts along dimension 0, may hold values from 3 to 64
- caption_blocks: int32 [8], P('grp'), parts along dimension 0, may hold values from 0 to 63, as said below
- header_slots: int32 [128, 2], P(('grp', 'seq')), parts along dimension 0, may hold values from 0 to 3
Outputs:
- grad_queries: bfloat16 [8192, 1024], P(('grp', 'seq'), 'head'), parts along dimension 0
- grad_keys: bfloat16 [8192, 1024], P(('grp', 'seq'), 'head'), parts along dimension 0
- grad_values: bfloat16 [8192, 1024], P(('grp', 'seq'), 'head'), parts along dimension 0
The draws below stay inside these ranges and needn't reach their ends.
There are 2 independent parts, one for each index of `grp`. The reference program is written for one: setup_inputs(seed, part) draws one part's arguments, and reference() takes and returns one part's arrays. A program takes and returns all parts, laid end to end along the dimension named above; each array names one. Nothing has to cross between parts.
Inputs may be any that keep to these rules, and one draw needn't show every extreme that they name: `caption_blocks`: 4 different block numbers, among them 0 and 63.
All inputs are finite; a program needn't handle non-finite values.
Results may differ from the reference program's by a relative error of at most 0.0095.
Values may be sent and summed in bfloat16 or wider, within the bound.
A program may use at most 64 MiB of HBM per device.

```python
import math
import jax
import jax.numpy as jnp
import numpy as np
from jax import lax

D = 1024
HEADS = 16
HEAD_DIM = 64
BLOCK = 64
RADIUS = 8
BLK_DEV = 8
CAP = 4
HDR = 2
NBLK = 64
CELLS = 4096
NTAB = 16
MOST = 32


def query_key_pair(key):
    base = jax.random.fold_in(key, 11)
    first_key, second_key = jax.random.split(base, 2)
    shape = (CELLS, D)
    query_draw = jax.random.truncated_normal(first_key, -4.0, 4.0, shape, jnp.float32)
    key_draw = jax.random.truncated_normal(second_key, -4.0, 4.0, shape, jnp.float32)
    return (query_draw, key_draw)


def draw_queries(key, part):
    return query_key_pair(key)[0].astype(jnp.bfloat16)


def draw_keys(key, part):
    return query_key_pair(key)[1].astype(jnp.bfloat16)


def draw_caption_blocks(key, part):
    first_key, second_key = jax.random.split(jax.random.fold_in(key, 23))
    inner = jax.random.permutation(first_key, NBLK - 2)[:CAP - 2].astype(jnp.int32) + 1
    chosen = jnp.concatenate([jnp.array([0, NBLK - 1], jnp.int32), inner])
    return jax.random.permutation(second_key, chosen).astype(jnp.int32)


def place_ends(drawn, key, low, top_value):
    dims = drawn.shape
    place = [jax.random.randint(jax.random.fold_in(key, axis), (), 0, dims[axis]) for axis in range(len(dims))]
    drawn = drawn.at[tuple(place)].set(low)
    longest = dims.index(max(dims))
    place[longest] = (place[longest] + 1) % dims[longest]
    return drawn.at[tuple(place)].set(top_value)


def level_of(stream_key, extent, pieces, least, top_value):
    factor_of, own = 1.0, jax.random.fold_in(stream_key, 6)
    for axis_at, shards_of in pieces:
        draws = jnp.exp(jax.random.uniform(jax.random.fold_in(own, axis_at), (shards_of,), jnp.float32, least / len(pieces), top_value / len(pieces)))
        factor_of = factor_of * jnp.repeat(draws, extent[axis_at] // shards_of).reshape([-1 if axis == axis_at else 1 for axis in range(len(extent))])
    return factor_of


def length_profile(amount, total, bound, skew):
    portions = [(1 << 20) // math.isqrt(standing ** skew) + 1 for standing in range(2, amount + 1)]
    surplus, counts = total - bound - (amount - 1), [1] * (amount - 1)
    while surplus > 0:
        movable = [i for i in range(amount - 1) if counts[i] < bound]
        whole, budget = sum([portions[i] for i in movable]), surplus
        for i in movable:
            addition = min(bound - counts[i], max(1, budget * portions[i] // whole), surplus)
            counts[i] = counts[i] + addition
            surplus = surplus - addition
    return np.array([bound] + counts)


def uneven(stream_key, amount, total, most, lean):
    if amount == 2:
        one = jax.random.randint(stream_key, (), max(1, total - most), min(most, total - 1) + 1)
        return jnp.stack([one, total - one])
    tallies = jnp.asarray(length_profile(amount, total, most, lean), jnp.int32)
    twos = (amount - 1) // 2
    source_of, sink = tallies[1:1 + 2 * twos:2], tallies[2:2 + 2 * twos:2]
    margin = jnp.minimum(source_of - 1, most - sink)
    passed = jax.random.randint(jax.random.fold_in(stream_key, 1), (twos,), 0, 1 << 20) % (margin + 1)
    tallies = tallies.at[1:1 + 2 * twos:2].set(source_of - passed).at[2:2 + 2 * twos:2].set(sink + passed)
    return tallies[jax.random.permutation(jax.random.fold_in(stream_key, 2), amount)]


def centred(stream_key, extent, spread, bound, shards=(), kind=jnp.bfloat16):
    entries = jax.random.normal(stream_key, extent, jnp.float32) * spread
    if len(shards) > 0:
        entries = level_of(stream_key, extent, shards, -0.22, 0.18) * entries
    return jnp.clip(entries, min=-bound, max=bound).astype(kind)


def setup_inputs(seed: int = 0, part: int = 0) -> dict:
    key_of = jax.random.split(jax.random.key(seed), 9)
    part_splits = jax.random.split(jax.random.fold_in(key_of[8], part), 9)
    return {
        "queries": draw_queries(jax.random.fold_in(jax.random.fold_in(key_of[8], part), 71), part),
        "keys": draw_keys(jax.random.fold_in(jax.random.fold_in(key_of[8], part), 71), part),
        "values": centred(part_splits[2], (CELLS, D), 1.0, 6.0, ((0, 8), (1, 2))),
        "grad_out": centred(part_splits[3], (CELLS, D), 1.0, 6.0, ((0, 8), (1, 2))),
        "table_lengths": uneven(part_splits[4], NTAB, NBLK, MOST, 2).astype(jnp.int32),
        "table_cols": place_ends(jax.random.randint(part_splits[5], (NTAB,), 3, 65), jax.random.fold_in(part_splits[5], 1), 3, 64).astype(jnp.int32),
        "caption_blocks": draw_caption_blocks(jax.random.fold_in(jax.random.fold_in(key_of[8], part), 71), part),
        "header_slots": place_ends(jax.random.randint(part_splits[7], (NBLK, HDR), 0, CAP), jax.random.fold_in(part_splits[7], 1), 0, CAP - 1).astype(jnp.int32),
    }


def cell_layout(cells, table_lengths, table_cols, total):
    lengths_cells = table_lengths * BLOCK
    starts = jnp.cumsum(lengths_cells, dtype=jnp.int32) - lengths_cells
    below = starts[None, :] <= cells[:, None]
    table_id = jnp.sum(below.astype(jnp.int32), axis=1, dtype=jnp.int32) - 1
    start_cell = jnp.max(jnp.where(below, starts[None, :], 0), axis=1)
    tables = jnp.arange(table_lengths.shape[0], dtype=jnp.int32)
    widths = jnp.sum(jnp.where(table_id[:, None] == tables[None, :], table_cols[None, :], 0), axis=1, dtype=jnp.int32)
    column = (cells - start_cell) % jnp.maximum(widths, 1)
    inside = (cells >= 0) & (cells < total)
    return table_id, cells - column, start_cell + column, inside


def visibility(query_cells, key_cells, table_lengths, table_cols, total):
    query_table, query_row, query_col, query_inside = cell_layout(query_cells, table_lengths, table_cols, total)
    key_table, key_row, key_col, key_inside = cell_layout(key_cells, table_lengths, table_cols, total)
    near = jnp.abs(query_cells[:, None] // BLOCK - key_cells[None, :] // BLOCK) <= RADIUS
    shared = (query_row[:, None] == key_row[None, :]) | (query_col[:, None] == key_col[None, :])
    same_table = query_table[:, None] == key_table[None, :]
    return same_table & shared & near & query_inside[:, None] & key_inside[None, :]


def attention_grads(query_rows, grad_rows, key_rows, value_rows, mask, scale):
    query_f = query_rows.astype(jnp.float32).reshape(-1, HEADS, HEAD_DIM)
    grad_f = grad_rows.astype(jnp.float32).reshape(-1, HEADS, HEAD_DIM)
    key_f = key_rows.astype(jnp.float32).reshape(-1, HEADS, HEAD_DIM)
    value_f = value_rows.astype(jnp.float32).reshape(-1, HEADS, HEAD_DIM)
    scores = jnp.einsum("qhd,khd->hqk", query_f, key_f) * scale
    scores = jnp.where(mask[None], scores, -1e30)
    top = jnp.max(scores, axis=2, keepdims=True)
    log_total = top + jnp.log(jnp.sum(jnp.exp(scores - top), axis=2, keepdims=True))
    probs = jnp.where(mask[None], jnp.exp(scores - log_total), 0.0)
    probs_low = lax.optimization_barrier(probs.astype(jnp.bfloat16)).astype(jnp.float32)
    outputs = jnp.einsum("hqk,khd->hqd", probs_low, value_f)
    delta = jnp.sum(jnp.transpose(grad_f, (1, 0, 2)) * outputs, axis=2, keepdims=True)
    grad_probs = jnp.einsum("qhd,khd->hqk", grad_f, value_f)
    grad_scores = (probs * (grad_probs - delta) * scale).astype(jnp.bfloat16)
    grad_scores = lax.optimization_barrier(grad_scores).astype(jnp.float32)
    grad_query = jnp.einsum("hqk,khd->qhd", grad_scores, key_f).reshape(-1, D)
    grad_key = jnp.einsum("hqk,qhd->khd", grad_scores, query_f).reshape(-1, D)
    grad_value = jnp.einsum("hqk,qhd->khd", probs_low, grad_f).reshape(-1, D)
    return grad_query, grad_key, grad_value


def reference(queries, keys, values, grad_out, table_lengths, table_cols, caption_blocks, header_slots):
    rows = BLK_DEV * BLOCK
    reach = RADIUS * BLOCK
    span = rows + 2 * reach
    total = CELLS
    scale = HEAD_DIM ** -0.5
    pair = jnp.stack([keys, values])
    padded = jnp.pad(pair, ((0, 0), (reach, reach), (0, 0)))
    caption_cells = (caption_blocks[:, None] * BLOCK + jnp.arange(BLOCK, dtype=jnp.int32)[None, :]).reshape(-1)
    caption_pair = jnp.take(pair, caption_cells, axis=1)
    listed = jnp.any(header_slots[:, :, None] == jnp.arange(CAP, dtype=jnp.int32)[None, None, :], axis=1)

    def group(carry, number):
        window_grads, caption_grads = carry
        first = number * rows
        own_cells = first + jnp.arange(rows, dtype=jnp.int32)
        window_cells = first - reach + jnp.arange(span, dtype=jnp.int32)
        query_rows = lax.dynamic_slice_in_dim(queries, first, rows, 0)
        grad_rows = lax.dynamic_slice_in_dim(grad_out, first, rows, 0)
        window_pair = lax.dynamic_slice_in_dim(padded, first, span, 1)
        window_mask = visibility(own_cells, window_cells, table_lengths, table_cols, total)
        block_list = lax.dynamic_slice_in_dim(listed, number * BLK_DEV, BLK_DEV, 0)
        caption_mask = jnp.repeat(jnp.repeat(block_list, BLOCK, axis=0), BLOCK, axis=1)
        mask = jnp.concatenate([window_mask, caption_mask], axis=1)
        key_all = jnp.concatenate([window_pair[0], caption_pair[0]], axis=0)
        value_all = jnp.concatenate([window_pair[1], caption_pair[1]], axis=0)
        grad_query, grad_key, grad_value = attention_grads(query_rows, grad_rows, key_all, value_all, mask, scale)
        pair_grads = jnp.stack([grad_key, grad_value])
        current = lax.dynamic_slice_in_dim(window_grads, first, span, 1)
        window_grads = lax.dynamic_update_slice_in_dim(window_grads, current + pair_grads[:, :span], first, 1)
        caption_grads = caption_grads + pair_grads[:, span:]
        return (window_grads, caption_grads), grad_query.astype(jnp.bfloat16)

    start = (jnp.zeros((2, CELLS + 2 * reach, D), jnp.float32), jnp.zeros((2, CAP * BLOCK, D), jnp.float32))
    (window_grads, caption_grads), grad_queries = lax.scan(group, start, jnp.arange(NBLK // BLK_DEV, dtype=jnp.int32))
    own = window_grads[:, reach:reach + CELLS]
    own = own.at[:, caption_cells].add(caption_grads)
    return grad_queries.reshape(CELLS, D), own[0].astype(jnp.bfloat16), own[1].astype(jnp.bfloat16)
```

```python
import functools

import jax
import jax.numpy as jnp
from jax import lax
from jax.experimental import pallas as pl
from jax.experimental.pallas import tpu as pltpu
from jax.sharding import PartitionSpec as P

HEAD_DIM = 64
BLOCK = 64
RADIUS = 8
LANES = 128
TILE = 256
HEADS_PER_PAIR = LANES // HEAD_DIM
NEG = -1e30
MESH = pl.DeviceIdType.MESH


def cell_ids(cells, lengths_ref, cols_ref, total):
    def step(table, carry):
        start, here, width = carry
        inside = cells >= start
        here = jnp.where(inside, start, here)
        width = jnp.where(inside, cols_ref[table], width)
        return (start + lengths_ref[table] * BLOCK, here, width)

    _, here, width = lax.fori_loop(
        0, lengths_ref.shape[0], step, (jnp.int32(0), jnp.zeros_like(cells), jnp.ones_like(cells))
    )
    offset = cells - here
    widthf = width.astype(jnp.float32)
    lines = jnp.floor((offset.astype(jnp.float32) + 0.5) / widthf).astype(jnp.int32)
    column = offset - lines * width
    inside = (cells >= 0) & (cells < total)
    return (
        jnp.where(inside, cells - column, -1),
        jnp.where(inside, here + column, -1),
    )


def kernel(
    n, lengths_ref, cols_ref, caps_ref, header_ref, q_ref, k_ref, v_ref, g_ref,
    dq_ref, dk_ref, dv_ref,
    win, acc, bias, kt, sbuf, dpbuf, plow, dsc, qs,
    far_out, far_in, near_out, near_in, piece, rs_in, full, gpiece, grs_in, gfull,
    a_send, a_recv, b_send, b_recv, c_send, c_recv, d_send, d_recv,
    e_send, e_recv, f_send, f_recv, x_send, x_recv, y_send, y_recv,
):
    rows, features = q_ref.shape
    pairs = features // LANES
    tiles = rows // TILE
    reach = RADIUS * BLOCK
    span = rows + 2 * reach
    wchunks = (TILE + 2 * reach) // TILE
    slots = caps_ref.shape[0]
    cap_rows = slots * BLOCK
    nchunk = wchunks + cap_rows // TILE
    reducers = 2 * slots
    me = lax.axis_index("seq")
    odd = me % 2
    partner = me + 1 - 2 * odd
    ahead = lax.rem(me + 2, n)
    behind = lax.rem(me + n - 2, n)
    high = reach + rows
    near_at = pl.multiple_of((1 - odd) * high, TILE)
    far_at = pl.multiple_of(odd * high, TILE)
    forward_to = jnp.where(odd == 1, behind, ahead)
    back_to = jnp.where(odd == 1, ahead, behind)
    kv = (k_ref, v_ref)

    def peers(body):
        def step(j, carry):
            body(j, lax.rem(me + j, n), lax.rem(me + n - j, n))
            return carry

        lax.fori_loop(1, n, step, 0)

    def guarded(index, body):
        if n == reducers:
            body()
        else:
            pl.when(index < reducers)(body)

    barrier = pltpu.get_barrier_semaphore()
    peers(lambda j, to, source: pl.semaphore_signal(
        barrier, inc=1, device_id={"seq": to}, device_id_type=MESH))
    pl.semaphore_wait(barrier, n - 1)

    def remote(src, dst, send, recv, to):
        return pltpu.make_async_remote_copy(
            src_ref=src, dst_ref=dst, send_sem=send, recv_sem=recv,
            device_id={"seq": to}, device_id_type=MESH)

    def lanes(p):
        return pl.ds(pl.multiple_of(p * LANES, LANES), LANES)

    def copy_a(c, p):
        return remote(kv[c].at[:, lanes(p)], win.at[c, p, pl.ds(far_at, rows)],
                      a_send.at[c, p], a_recv.at[c, p], partner)

    def copy_b(c, p):
        return remote(win.at[c, p, pl.ds(near_at, rows)], win.at[c, p, pl.ds(far_at, rows)],
                      b_send.at[c, p], b_recv.at[c, p], forward_to)

    def copy_c(c, p):
        return remote(far_out.at[c, p], far_in.at[c, p], c_send.at[c, p], c_recv.at[c, p], back_to)

    def copy_d(c, p):
        return remote(near_out.at[c, p], near_in.at[c, p], d_send.at[c, p], d_recv.at[c, p], partner)

    def scatter(source_buf, dest, send, recv, j, to):
        return remote(source_buf.at[to], dest.at[me], send.at[j], recv.at[j], to)

    def gather(buf, send, recv, j, to):
        return remote(buf.at[me], buf.at[me], send.at[j], recv.at[j], to)

    def start_scatter(source_buf, dest, send, recv):
        peers(lambda j, to, source: guarded(
            to, lambda: scatter(source_buf, dest, send, recv, j, to).start()))

    def reduce_and_gather(source_buf, dest, out, send, recv, gsend, grecv):
        def mine():
            peers(lambda j, to, source: scatter(source_buf, dest, send, recv, j, to).wait_recv())
            total = source_buf[me].astype(jnp.float32)

            def add(j, value):
                return value + dest[lax.rem(me + j, n)].astype(jnp.float32)

            out[me] = lax.fori_loop(1, n, add, total).astype(jnp.bfloat16)
            peers(lambda j, to, source: gather(out, gsend, grecv, j, to).start())

        guarded(me, mine)

    def wait_gather(source_buf, dest, out, send, recv, gsend, grecv):
        peers(lambda j, to, source: guarded(
            source, lambda: gather(out, gsend, grecv, j, to).wait_recv()))
        guarded(me, lambda: peers(
            lambda j, to, source: gather(out, gsend, grecv, j, to).wait_send()))
        peers(lambda j, to, source: guarded(
            to, lambda: scatter(source_buf, dest, send, recv, j, to).wait_send()))

    blocks_here = rows // BLOCK
    for s in range(slots):
        owned = [
            jnp.where(caps_ref[s] == me * blocks_here + b, 1.0, 0.0).astype(jnp.bfloat16)
            for b in range(blocks_here)
        ]
        for c in range(2):
            offer = kv[c][:BLOCK] * owned[0]
            for b in range(1, blocks_here):
                offer = offer + kv[c][b * BLOCK:(b + 1) * BLOCK] * owned[b]
            piece[c * slots + s] = offer
    start_scatter(piece, rs_in, e_send, e_recv)
    for p in range(pairs):
        for c in range(2):
            copy_a(c, p).start()

    for p in range(pairs):
        for c in range(2):
            win[c, p, pl.ds(reach, rows)] = kv[c][:, p * LANES:(p + 1) * LANES]

    total_cells = lax.fori_loop(
        0, lengths_ref.shape[0], lambda t, value: value + lengths_ref[t] * BLOCK, jnp.int32(0))
    first = me * rows
    query_ids = []
    for t in range(tiles):
        cells = first + t * TILE + lax.broadcasted_iota(jnp.int32, (8, TILE), 1)
        row, col = cell_ids(cells, lengths_ref, cols_ref, total_cells)
        query_ids.append((row[:1], col[:1], cells[:1] // BLOCK))

    for chunk in range(span // TILE):
        cells = first - reach + chunk * TILE + lax.broadcasted_iota(jnp.int32, (TILE, LANES), 0)
        row, col = cell_ids(cells, lengths_ref, cols_ref, total_cells)
        key_block = (cells + reach) // BLOCK - RADIUS
        row, col, key_block = (
            jnp.concatenate([x] * (TILE // LANES), axis=1) for x in (row, col, key_block))
        for t in range(tiles):
            if 0 <= chunk - t < wchunks:
                qrow, qcol, qblock = query_ids[t]
                near = jnp.abs(key_block - qblock) <= RADIUS
                seen = near & ((row == qrow) | (col == qcol))
                bias[t, (chunk - t) * TILE:(chunk - t + 1) * TILE] = jnp.where(seen, 0.0, NEG)
    for t in range(tiles):
        local = (t * TILE + lax.broadcasted_iota(jnp.int32, (1, TILE), 1)) // BLOCK
        for s in range(slots):
            line = jnp.full((1, TILE), NEG, jnp.float32)
            for b in range(t * TILE // BLOCK, (t + 1) * TILE // BLOCK):
                hit = header_ref[b, 0] == s
                for extra in range(1, header_ref.shape[1]):
                    hit = hit | (header_ref[b, extra] == s)
                line = jnp.where(local == b, jnp.where(hit, 0.0, NEG), line)
            at = wchunks * TILE + s * BLOCK
            bias[t, at:at + BLOCK] = jnp.broadcast_to(line, (BLOCK, TILE))

    reduce_and_gather(piece, rs_in, full, e_send, e_recv, f_send, f_recv)
    for c in range(2):
        copy_a(c, 0).wait_recv()
        copy_b(c, 0).start()
    wait_gather(piece, rs_in, full, e_send, e_recv, f_send, f_recv)
    for p in range(pairs):
        for c in range(2):
            for s in range(slots):
                win[c, p, span + s * BLOCK:span + (s + 1) * BLOCK] = (
                    full[c * slots + s, :, p * LANES:(p + 1) * LANES])

    lane = lax.broadcasted_iota(jnp.int32, (TILE, LANES), 1) // HEAD_DIM

    def fold(x, op):
        return op(x.reshape(TILE // 8, 8, TILE), axis=0)

    def compute(p):
        acc[:, p] = jnp.zeros_like(acc[:, p])
        kt[...] = win[0, p].T

        def tile(t, carry):
            q_rows = pl.ds(pl.multiple_of(t * TILE, TILE), TILE)
            q = q_ref[q_rows, lanes(p)] * jnp.bfloat16(HEAD_DIM ** -0.5)
            g = g_ref[q_rows, lanes(p)]
            starts = [pl.multiple_of(t * TILE + i * TILE, TILE) for i in range(wchunks)]
            starts += [span + i * TILE for i in range(cap_rows // TILE)]
            zero = jnp.zeros_like(q)
            nt = (((1,), (1,)), ((), ()))
            grad_q = []
            for h in range(HEADS_PER_PAIR):
                qh = jnp.where(lane == h, q, zero)
                gh = jnp.where(lane == h, g, zero)
                qs[0, h * TILE:(h + 1) * TILE] = qh
                qs[1, h * TILE:(h + 1) * TILE] = gh
                top = jnp.full((8, TILE), NEG, jnp.float32)
                for i, at in enumerate(starts):
                    r = slice(i * TILE, (i + 1) * TILE)
                    scores = lax.dot_general(win[0, p, pl.ds(at, TILE)], qh, nt,
                                             preferred_element_type=jnp.float32) + bias[t, r]
                    sbuf[h, r] = scores
                    top = jnp.maximum(top, fold(scores, jnp.max))
                top = jnp.max(top, axis=0, keepdims=True)
                norm = jnp.zeros((8, TILE), jnp.float32)
                for i, at in enumerate(starts):
                    r = slice(i * TILE, (i + 1) * TILE)
                    e = jnp.exp(sbuf[h, r] - top)
                    sbuf[h, r] = e
                    norm = norm + fold(e, jnp.sum)
                inverse = 1.0 / jnp.sum(norm, axis=0, keepdims=True)
                delta = jnp.zeros((8, TILE), jnp.float32)
                for i, at in enumerate(starts):
                    r = slice(i * TILE, (i + 1) * TILE)
                    probs = sbuf[h, r] * inverse
                    sbuf[h, r] = probs
                    low = probs.astype(jnp.bfloat16)
                    plow[r, h * TILE:(h + 1) * TILE] = low
                    dp = lax.dot_general(win[1, p, pl.ds(at, TILE)], gh, nt,
                                         preferred_element_type=jnp.float32)
                    dpbuf[h, r] = dp
                    delta = delta + fold(low.astype(jnp.float32) * dp, jnp.sum)
                delta = jnp.sum(delta, axis=0, keepdims=True)
                gq = jnp.zeros((HEAD_DIM, TILE), jnp.float32)
                for i, at in enumerate(starts):
                    r = slice(i * TILE, (i + 1) * TILE)
                    ds = (sbuf[h, r] * (dpbuf[h, r] - delta)).astype(jnp.bfloat16)
                    dsc[r, h * TILE:(h + 1) * TILE] = ds
                    gq = gq + jnp.dot(kt[h * HEAD_DIM:(h + 1) * HEAD_DIM, pl.ds(at, TILE)], ds,
                                      preferred_element_type=jnp.float32)
                grad_q.append(gq)
            for i, at in enumerate(starts):
                r = slice(i * TILE, (i + 1) * TILE)
                acc[0, p, pl.ds(at, TILE)] += jnp.dot(
                    dsc[r], qs[0], preferred_element_type=jnp.float32)
                acc[1, p, pl.ds(at, TILE)] += jnp.dot(
                    plow[r], qs[1], preferred_element_type=jnp.float32)
            joined = jnp.concatenate(grad_q, axis=0) * (HEAD_DIM ** -0.5)
            dq_ref[q_rows, lanes(p)] = joined.T.astype(jnp.bfloat16)
            return carry

        lax.fori_loop(0, tiles, tile, 0)

    def combine(p):
        for c in range(2):
            copy_c(c, p).wait_recv()
            near_out[c, p] = (acc[c, p, pl.ds(near_at, rows)]
                              + far_in[c, p].astype(jnp.float32)).astype(jnp.bfloat16)
            copy_d(c, p).start()

    def pair(p, carry):
        @pl.when(p + 1 < pairs)
        def _():
            for c in range(2):
                copy_a(c, p + 1).wait_recv()
                copy_b(c, p + 1).start()

        for c in range(2):
            copy_b(c, p).wait_recv()
        compute(p)
        for c in range(2):
            far_out[c, p] = acc[c, p, pl.ds(far_at, rows)].astype(jnp.bfloat16)
            copy_c(c, p).start()
            for s in range(slots):
                gpiece[c * slots + s, :, lanes(p)] = acc[
                    c, p, span + s * BLOCK:span + (s + 1) * BLOCK].astype(jnp.bfloat16)

        @pl.when(p >= 1)
        def _():
            combine(p - 1)

        return carry

    lax.fori_loop(0, pairs, pair, 0)
    start_scatter(gpiece, grs_in, x_send, x_recv)
    combine(pairs - 1)
    reduce_and_gather(gpiece, grs_in, gfull, x_send, x_recv, y_send, y_recv)
    outs = (dk_ref, dv_ref)
    for p in range(pairs):
        for c in range(2):
            copy_d(c, p).wait_recv()
            acc[c, p, pl.ds(reach, rows)] += near_in[c, p].astype(jnp.float32)
    wait_gather(gpiece, grs_in, gfull, x_send, x_recv, y_send, y_recv)
    for b in range(blocks_here):
        weights = [jnp.where(caps_ref[s] == me * blocks_here + b, 1.0, 0.0) for s in range(slots)]
        r = slice(b * BLOCK, (b + 1) * BLOCK)
        for c in range(2):
            for p in range(pairs):
                ls = slice(p * LANES, (p + 1) * LANES)
                value = acc[c, p, reach + b * BLOCK:reach + (b + 1) * BLOCK]
                for s in range(slots):
                    value = value + gfull[c * slots + s, :, ls].astype(jnp.float32) * weights[s]
                outs[c][r, ls] = value.astype(jnp.bfloat16)
    for p in range(pairs):
        for c in range(2):
            copy_a(c, p).wait_send()
            copy_b(c, p).wait_send()
            copy_c(c, p).wait_send()
            copy_d(c, p).wait_send()


def shards(
    queries, keys, values, grad_out, table_lengths, table_cols, caption_blocks, header_slots
):
    n = lax.axis_size("seq")
    rows, features = queries.shape
    pairs = features // LANES
    tiles = rows // TILE
    slots = caption_blocks.shape[0]
    reducers = 2 * slots
    span = rows + 2 * RADIUS * BLOCK
    keys_all = span + slots * BLOCK
    seen_rows = TILE + 2 * RADIUS * BLOCK + slots * BLOCK
    bf16, f32 = jnp.bfloat16, jnp.float32
    vmem = pl.BlockSpec(memory_space=pltpu.VMEM)
    smem = pl.BlockSpec(memory_space=pltpu.SMEM)
    out = jax.ShapeDtypeStruct((rows, features), bf16)
    pair_sem = pltpu.SemaphoreType.DMA((2, pairs))
    peer_sem = pltpu.SemaphoreType.DMA((n,))
    halo = pltpu.VMEM((2, pairs, rows, LANES), bf16)
    chunks = pltpu.VMEM((reducers, BLOCK, features), bf16)
    arrivals = pltpu.VMEM((n, BLOCK, features), bf16)
    return pl.pallas_call(
        functools.partial(kernel, n),
        out_shape=(out, out, out),
        in_specs=[smem] * 4 + [vmem] * 4,
        out_specs=(vmem, vmem, vmem),
        scratch_shapes=[
            pltpu.VMEM((2, pairs, keys_all, LANES), bf16),
            pltpu.VMEM((2, pairs, keys_all, LANES), f32),
            pltpu.VMEM((tiles, seen_rows, TILE), f32),
            pltpu.VMEM((LANES, keys_all), bf16),
            pltpu.VMEM((HEADS_PER_PAIR, seen_rows, TILE), f32),
            pltpu.VMEM((HEADS_PER_PAIR, seen_rows, TILE), f32),
            pltpu.VMEM((seen_rows, HEADS_PER_PAIR * TILE), bf16),
            pltpu.VMEM((seen_rows, HEADS_PER_PAIR * TILE), bf16),
            pltpu.VMEM((2, HEADS_PER_PAIR * TILE, LANES), bf16),
            halo, halo, halo, halo,
            chunks, arrivals, chunks, chunks, arrivals, chunks,
        ] + [pair_sem] * 8 + [peer_sem] * 8,
        compiler_params=pltpu.CompilerParams(
            collective_id=0, has_side_effects=True, vmem_limit_bytes=56 * 2**20),
        cost_estimate=pl.CostEstimate(
            flops=10 * rows * seen_rows * features, transcendentals=rows * seen_rows * 8,
            bytes_accessed=14 * rows * features),
    )(table_lengths, table_cols, caption_blocks, header_slots, queries, keys, values, grad_out)


def solution(mesh):
    band = P(("grp", "seq"), "head")
    return jax.shard_map(
        shards,
        mesh=mesh,
        in_specs=(band, band, band, band, P("grp"), P("grp"), P("grp"), P(("grp", "seq"), None)),
        out_specs=(band, band, band),
        check_vma=False,
    )
```

```python
import functools

import jax
import jax.numpy as jnp
from jax import lax
from jax.experimental import pallas as pl
from jax.experimental.pallas import tpu as pltpu
from jax.sharding import PartitionSpec as P

HEAD_DIM = 64
BLOCK = 64
RADIUS = 8
LANES = 128
TILE = 256
HEADS_PER_PAIR = LANES // HEAD_DIM
NEG = -1e30
MESH = pl.DeviceIdType.MESH


def cell_ids(cells, lengths_ref, cols_ref, total):
    def step(table, carry):
        start, here, width = carry
        inside = cells >= start
        here = jnp.where(inside, start, here)
        width = jnp.where(inside, cols_ref[table], width)
        return (start + lengths_ref[table] * BLOCK, here, width)

    _, here, width = lax.fori_loop(
        0, lengths_ref.shape[0], step, (jnp.int32(0), jnp.zeros_like(cells), jnp.ones_like(cells))
    )
    offset = cells - here
    widthf = width.astype(jnp.float32)
    lines = jnp.floor((offset.astype(jnp.float32) + 0.5) / widthf).astype(jnp.int32)
    column = offset - lines * width
    inside = (cells >= 0) & (cells < total)
    return (
        jnp.where(inside, cells - column, -1),
        jnp.where(inside, here + column, -1),
    )


def kernel(
    n, lengths_ref, cols_ref, caps_ref, header_ref, q_ref, k_ref, v_ref, g_ref,
    dq_ref, dk_ref, dv_ref,
    win, acc, bias, kt, sbuf, dpbuf, plow, dsc, qs,
    far_out, far_in, near_out, near_in, piece, rs_in, full, gpiece, grs_in, gfull,
    a_send, a_recv, b_send, b_recv, c_send, c_recv, d_send, d_recv,
    e_send, e_recv, f_send, f_recv, x_send, x_recv, y_send, y_recv,
):
    rows, features = q_ref.shape
    pairs = features // LANES
    tiles = rows // TILE
    reach = RADIUS * BLOCK
    span = rows + 2 * reach
    wchunks = (TILE + 2 * reach) // TILE
    slots = caps_ref.shape[0]
    cap_rows = slots * BLOCK
    nchunk = wchunks + cap_rows // TILE
    reducers = 2 * slots
    me = lax.axis_index("seq")
    odd = me % 2
    partner = me + 1 - 2 * odd
    ahead = lax.rem(me + 2, n)
    behind = lax.rem(me + n - 2, n)
    high = reach + rows
    near_at = pl.multiple_of((1 - odd) * high, TILE)
    far_at = pl.multiple_of(odd * high, TILE)
    forward_to = jnp.where(odd == 1, behind, ahead)
    back_to = jnp.where(odd == 1, ahead, behind)
    kv = (k_ref, v_ref)

    def peers(body):
        def step(j, carry):
            body(j, lax.rem(me + j, n), lax.rem(me + n - j, n))
            return carry

        lax.fori_loop(1, n, step, 0)

    def guarded(index, body):
        if n == reducers:
            body()
        else:
            pl.when(index < reducers)(body)

    barrier = pltpu.get_barrier_semaphore()
    peers(lambda j, to, source: pl.semaphore_signal(
        barrier, inc=1, device_id={"seq": to}, device_id_type=MESH))
    pl.semaphore_wait(barrier, n - 1)

    def remote(src, dst, send, recv, to):
        return pltpu.make_async_remote_copy(
            src_ref=src, dst_ref=dst, send_sem=send, recv_sem=recv,
            device_id={"seq": to}, device_id_type=MESH)

    def lanes(p):
        return pl.ds(pl.multiple_of(p * LANES, LANES), LANES)

    def copy_a(c, p):
        return remote(kv[c].at[:, lanes(p)], win.at[c, p, pl.ds(far_at, rows)],
                      a_send.at[c, p], a_recv.at[c, p], partner)

    def copy_b(c, p):
        return remote(win.at[c, p, pl.ds(near_at, rows)], win.at[c, p, pl.ds(far_at, rows)],
                      b_send.at[c, p], b_recv.at[c, p], forward_to)

    def copy_c(c, p):
        return remote(far_out.at[c, p], far_in.at[c, p], c_send.at[c, p], c_recv.at[c, p], back_to)

    def copy_d(c, p):
        return remote(near_out.at[c, p], near_in.at[c, p], d_send.at[c, p], d_recv.at[c, p], partner)

    def scatter(source_buf, dest, send, recv, j, to):
        return remote(source_buf.at[to], dest.at[me], send.at[j], recv.at[j], to)

    def gather(buf, send, recv, j, to):
        return remote(buf.at[me], buf.at[me], send.at[j], recv.at[j], to)

    def start_scatter(source_buf, dest, send, recv):
        peers(lambda j, to, source: guarded(
            to, lambda: scatter(source_buf, dest, send, recv, j, to).start()))

    def reduce_and_gather(source_buf, dest, out, send, recv, gsend, grecv):
        def mine():
            peers(lambda j, to, source: scatter(source_buf, dest, send, recv, j, to).wait_recv())
            total = source_buf[me].astype(jnp.float32)

            def add(j, value):
                return value + dest[lax.rem(me + j, n)].astype(jnp.float32)

            out[me] = lax.fori_loop(1, n, add, total).astype(jnp.bfloat16)
            peers(lambda j, to, source: gather(out, gsend, grecv, j, to).start())

        guarded(me, mine)

    def wait_gather(source_buf, dest, out, send, recv, gsend, grecv):
        peers(lambda j, to, source: guarded(
            source, lambda: gather(out, gsend, grecv, j, to).wait_recv()))
        guarded(me, lambda: peers(
            lambda j, to, source: gather(out, gsend, grecv, j, to).wait_send()))
        peers(lambda j, to, source: guarded(
            to, lambda: scatter(source_buf, dest, send, recv, j, to).wait_send()))

    blocks_here = rows // BLOCK
    for s in range(slots):
        owned = [
            jnp.where(caps_ref[s] == me * blocks_here + b, 1.0, 0.0).astype(jnp.bfloat16)
            for b in range(blocks_here)
        ]
        for c in range(2):
            offer = kv[c][:BLOCK] * owned[0]
            for b in range(1, blocks_here):
                offer = offer + kv[c][b * BLOCK:(b + 1) * BLOCK] * owned[b]
            piece[c * slots + s] = offer
    start_scatter(piece, rs_in, e_send, e_recv)
    for c in range(2):
        copy_a(c, 0).start()

    for p in range(pairs):
        for c in range(2):
            win[c, p, pl.ds(reach, rows)] = kv[c][:, p * LANES:(p + 1) * LANES]

    total_cells = lax.fori_loop(
        0, lengths_ref.shape[0], lambda t, value: value + lengths_ref[t] * BLOCK, jnp.int32(0))
    first = me * rows
    query_ids = []
    for t in range(tiles):
        cells = first + t * TILE + lax.broadcasted_iota(jnp.int32, (8, TILE), 1)
        row, col = cell_ids(cells, lengths_ref, cols_ref, total_cells)
        query_ids.append((row[:1], col[:1], cells[:1] // BLOCK))

    reduce_and_gather(piece, rs_in, full, e_send, e_recv, f_send, f_recv)
    for chunk in range(span // TILE):
        cells = first - reach + chunk * TILE + lax.broadcasted_iota(jnp.int32, (TILE, LANES), 0)
        row, col = cell_ids(cells, lengths_ref, cols_ref, total_cells)
        key_block = (cells + reach) // BLOCK - RADIUS
        row, col, key_block = (
            jnp.concatenate([x] * (TILE // LANES), axis=1) for x in (row, col, key_block))
        for t in range(tiles):
            if 0 <= chunk - t < wchunks:
                qrow, qcol, qblock = query_ids[t]
                near = jnp.abs(key_block - qblock) <= RADIUS
                seen = near & ((row == qrow) | (col == qcol))
                bias[t, (chunk - t) * TILE:(chunk - t + 1) * TILE] = jnp.where(seen, 0.0, NEG)
    for t in range(tiles):
        local = (t * TILE + lax.broadcasted_iota(jnp.int32, (1, TILE), 1)) // BLOCK
        for s in range(slots):
            line = jnp.full((1, TILE), NEG, jnp.float32)
            for b in range(t * TILE // BLOCK, (t + 1) * TILE // BLOCK):
                hit = header_ref[b, 0] == s
                for extra in range(1, header_ref.shape[1]):
                    hit = hit | (header_ref[b, extra] == s)
                line = jnp.where(local == b, jnp.where(hit, 0.0, NEG), line)
            at = wchunks * TILE + s * BLOCK
            bias[t, at:at + BLOCK] = jnp.broadcast_to(line, (BLOCK, TILE))

    for c in range(2):
        copy_a(c, 0).wait_recv()
        copy_b(c, 0).start()
    wait_gather(piece, rs_in, full, e_send, e_recv, f_send, f_recv)
    for p in range(1, pairs):
        for c in range(2):
            copy_a(c, p).start()
    for p in range(pairs):
        for c in range(2):
            for s in range(slots):
                win[c, p, span + s * BLOCK:span + (s + 1) * BLOCK] = (
                    full[c * slots + s, :, p * LANES:(p + 1) * LANES])

    lane = lax.broadcasted_iota(jnp.int32, (TILE, LANES), 1) // HEAD_DIM

    def fold(x, op):
        return op(x.reshape(TILE // 8, 8, TILE), axis=0)

    def compute(p):
        acc[:, p] = jnp.zeros_like(acc[:, p])
        kt[...] = win[0, p].T

        def tile(t, carry):
            q_rows = pl.ds(pl.multiple_of(t * TILE, TILE), TILE)
            q = q_ref[q_rows, lanes(p)] * jnp.bfloat16(HEAD_DIM ** -0.5)
            g = g_ref[q_rows, lanes(p)]
            starts = [pl.multiple_of(t * TILE + i * TILE, TILE) for i in range(wchunks)]
            starts += [span + i * TILE for i in range(cap_rows // TILE)]
            zero = jnp.zeros_like(q)
            nt = (((1,), (1,)), ((), ()))
            grad_q = []
            for h in range(HEADS_PER_PAIR):
                qh = jnp.where(lane == h, q, zero)
                gh = jnp.where(lane == h, g, zero)
                qs[0, h * TILE:(h + 1) * TILE] = qh
                qs[1, h * TILE:(h + 1) * TILE] = gh
                top = jnp.full((8, TILE), NEG, jnp.float32)
                for i, at in enumerate(starts):
                    r = slice(i * TILE, (i + 1) * TILE)
                    scores = lax.dot_general(win[0, p, pl.ds(at, TILE)], qh, nt,
                                             preferred_element_type=jnp.float32) + bias[t, r]
                    sbuf[h, r] = scores
                    top = jnp.maximum(top, fold(scores, jnp.max))
                top = jnp.max(top, axis=0, keepdims=True)
                norm = jnp.zeros((8, TILE), jnp.float32)
                for i, at in enumerate(starts):
                    r = slice(i * TILE, (i + 1) * TILE)
                    e = jnp.exp(sbuf[h, r] - top)
                    sbuf[h, r] = e
                    norm = norm + fold(e, jnp.sum)
                inverse = 1.0 / jnp.sum(norm, axis=0, keepdims=True)
                delta = jnp.zeros((8, TILE), jnp.float32)
                for i, at in enumerate(starts):
                    r = slice(i * TILE, (i + 1) * TILE)
                    probs = sbuf[h, r] * inverse
                    sbuf[h, r] = probs
                    low = probs.astype(jnp.bfloat16)
                    plow[r, h * TILE:(h + 1) * TILE] = low
                    dp = lax.dot_general(win[1, p, pl.ds(at, TILE)], gh, nt,
                                         preferred_element_type=jnp.float32)
                    dpbuf[h, r] = dp
                    delta = delta + fold(low.astype(jnp.float32) * dp, jnp.sum)
                delta = jnp.sum(delta, axis=0, keepdims=True)
                gq = jnp.zeros((HEAD_DIM, TILE), jnp.float32)
                for i, at in enumerate(starts):
                    r = slice(i * TILE, (i + 1) * TILE)
                    ds = (sbuf[h, r] * (dpbuf[h, r] - delta)).astype(jnp.bfloat16)
                    dsc[r, h * TILE:(h + 1) * TILE] = ds
                    gq = gq + jnp.dot(kt[h * HEAD_DIM:(h + 1) * HEAD_DIM, pl.ds(at, TILE)], ds,
                                      preferred_element_type=jnp.float32)
                grad_q.append(gq)
            for i, at in enumerate(starts):
                r = slice(i * TILE, (i + 1) * TILE)
                acc[0, p, pl.ds(at, TILE)] += jnp.dot(
                    dsc[r], qs[0], preferred_element_type=jnp.float32)
                acc[1, p, pl.ds(at, TILE)] += jnp.dot(
                    plow[r], qs[1], preferred_element_type=jnp.float32)
            joined = jnp.concatenate(grad_q, axis=0) * (HEAD_DIM ** -0.5)
            dq_ref[q_rows, lanes(p)] = joined.T.astype(jnp.bfloat16)
            return carry

        lax.fori_loop(0, tiles, tile, 0)

    def combine(p):
        for c in range(2):
            copy_c(c, p).wait_recv()
            near_out[c, p] = (acc[c, p, pl.ds(near_at, rows)]
                              + far_in[c, p].astype(jnp.float32)).astype(jnp.bfloat16)
            copy_d(c, p).start()

    def pair(p, carry):
        @pl.when(p + 1 < pairs)
        def _():
            for c in range(2):
                copy_a(c, p + 1).wait_recv()
                copy_b(c, p + 1).start()

        for c in range(2):
            copy_b(c, p).wait_recv()
        compute(p)
        for c in range(2):
            far_out[c, p] = acc[c, p, pl.ds(far_at, rows)].astype(jnp.bfloat16)
            copy_c(c, p).start()
            for s in range(slots):
                gpiece[c * slots + s, :, lanes(p)] = acc[
                    c, p, span + s * BLOCK:span + (s + 1) * BLOCK].astype(jnp.bfloat16)

        @pl.when(p >= 1)
        def _():
            combine(p - 1)

        return carry

    lax.fori_loop(0, pairs, pair, 0)
    start_scatter(gpiece, grs_in, x_send, x_recv)
    combine(pairs - 1)
    reduce_and_gather(gpiece, grs_in, gfull, x_send, x_recv, y_send, y_recv)
    outs = (dk_ref, dv_ref)
    for p in range(pairs):
        for c in range(2):
            copy_d(c, p).wait_recv()
            acc[c, p, pl.ds(reach, rows)] += near_in[c, p].astype(jnp.float32)
    wait_gather(gpiece, grs_in, gfull, x_send, x_recv, y_send, y_recv)
    for b in range(blocks_here):
        weights = [jnp.where(caps_ref[s] == me * blocks_here + b, 1.0, 0.0) for s in range(slots)]
        r = slice(b * BLOCK, (b + 1) * BLOCK)
        for c in range(2):
            for p in range(pairs):
                ls = slice(p * LANES, (p + 1) * LANES)
                value = acc[c, p, reach + b * BLOCK:reach + (b + 1) * BLOCK]
                for s in range(slots):
                    value = value + gfull[c * slots + s, :, ls].astype(jnp.float32) * weights[s]
                outs[c][r, ls] = value.astype(jnp.bfloat16)
    for p in range(pairs):
        for c in range(2):
            copy_a(c, p).wait_send()
            copy_b(c, p).wait_send()
            copy_c(c, p).wait_send()
            copy_d(c, p).wait_send()


def shards(
    queries, keys, values, grad_out, table_lengths, table_cols, caption_blocks, header_slots
):
    n = lax.axis_size("seq")
    rows, features = queries.shape
    pairs = features // LANES
    tiles = rows // TILE
    slots = caption_blocks.shape[0]
    reducers = 2 * slots
    span = rows + 2 * RADIUS * BLOCK
    keys_all = span + slots * BLOCK
    seen_rows = TILE + 2 * RADIUS * BLOCK + slots * BLOCK
    bf16, f32 = jnp.bfloat16, jnp.float32
    vmem = pl.BlockSpec(memory_space=pltpu.VMEM)
    smem = pl.BlockSpec(memory_space=pltpu.SMEM)
    out = jax.ShapeDtypeStruct((rows, features), bf16)
    pair_sem = pltpu.SemaphoreType.DMA((2, pairs))
    peer_sem = pltpu.SemaphoreType.DMA((n,))
    halo = pltpu.VMEM((2, pairs, rows, LANES), bf16)
    chunks = pltpu.VMEM((reducers, BLOCK, features), bf16)
    arrivals = pltpu.VMEM((n, BLOCK, features), bf16)
    return pl.pallas_call(
        functools.partial(kernel, n),
        out_shape=(out, out, out),
        in_specs=[smem] * 4 + [vmem] * 4,
        out_specs=(vmem, vmem, vmem),
        scratch_shapes=[
            pltpu.VMEM((2, pairs, keys_all, LANES), bf16),
            pltpu.VMEM((2, pairs, keys_all, LANES), f32),
            pltpu.VMEM((tiles, seen_rows, TILE), f32),
            pltpu.VMEM((LANES, keys_all), bf16),
            pltpu.VMEM((HEADS_PER_PAIR, seen_rows, TILE), f32),
            pltpu.VMEM((HEADS_PER_PAIR, seen_rows, TILE), f32),
            pltpu.VMEM((seen_rows, HEADS_PER_PAIR * TILE), bf16),
            pltpu.VMEM((seen_rows, HEADS_PER_PAIR * TILE), bf16),
            pltpu.VMEM((2, HEADS_PER_PAIR * TILE, LANES), bf16),
            halo, halo, halo, halo,
            chunks, arrivals, chunks, chunks, arrivals, chunks,
        ] + [pair_sem] * 8 + [peer_sem] * 8,
        compiler_params=pltpu.CompilerParams(
            collective_id=0, has_side_effects=True, vmem_limit_bytes=56 * 2**20),
        cost_estimate=pl.CostEstimate(
            flops=10 * rows * seen_rows * features, transcendentals=rows * seen_rows * 8,
            bytes_accessed=14 * rows * features),
    )(table_lengths, table_cols, caption_blocks, header_slots, queries, keys, values, grad_out)


def solution(mesh):
    band = P(("grp", "seq"), "head")
    return jax.shard_map(
        shards,
        mesh=mesh,
        in_specs=(band, band, band, band, P("grp"), P("grp"), P("grp"), P(("grp", "seq"), None)),
        out_specs=(band, band, band),
        check_vma=False,
    )
```
